32 devices in a mesh: leaf: 8 (over z, x), sep: 4 (over y, core).
Axes of the slice: x: 2, y: 2, z: 4, core: 2. Of those that a mesh axis runs over, the one named last changes fastest.
Arguments:
- right_side: float32 [32768, 128], P(('leaf', 'sep')), may hold values from -6 to 6
- inverse_root: bfloat16 [8192, 8192], P(('leaf', 'sep')), may hold values from -1 to 3
- inverse_middle: bfloat16 [8192, 4096], P(('leaf', 'sep')), may hold values from -1 to 3
- inverse_lower: bfloat16 [16384, 4096], P(('leaf', 'sep')), may hold values from -1 to 3
- update_middle: bfloat16 [8192, 128], P(('leaf', 'sep')), may hold values from -0.09375 to 0.09375
- update_lower: bfloat16 [16384, 64], P(('leaf', 'sep')), may hold values from -0.09375 to 0.09375
- target_middle: int32 [32, 1], P(('leaf', 'sep')), may hold values from 0 to 31
- target_lower: int32 [32, 1], P(('leaf', 'sep')), may hold values from 0 to 63
Outputs:
- solution: float32 [32768, 128], P(('leaf', 'sep'))
The draws below stay inside these ranges and needn't reach their ends.
All inputs are finite; a program needn't handle non-finite values.
Results may differ from the reference program's by a relative error of at most 0.0037.
Values may be sent and summed in bfloat16 or wider, within the bound.
A program may use at most 64 MiB of HBM per device.

```python
import math
import jax
import jax.numpy as jnp

ROOT_ROWS = 8192
SEP_ROWS = 4096
RHS = 128
BLOCK = 8
SLOTS = 1
DEV_ROWS = 256
MID_UPD = 128
LOW_UPD = 64
N_LEAF = 8
N_SEP = 4


def dominant(key, rows, cols):
    first, second = jax.random.split(key)
    column = jnp.arange(cols, dtype=jnp.int32)[None, :]
    row = (jnp.arange(rows, dtype=jnp.int32) % cols)[:, None]
    diagonal = jnp.exp(jax.random.uniform(first, (rows, 1), jnp.float32, math.log(0.5), math.log(2.0)))
    spread = jnp.clip(jax.random.normal(second, (rows, cols), jnp.float32), -6.0, 6.0) * (1.5 / math.sqrt(cols))
    return jnp.where(row == column, diagonal, spread).astype(jnp.bfloat16)


def draw_inverse_root(key, part):
    return dominant(key, ROOT_ROWS, ROOT_ROWS)


def draw_inverse_middle(key, part):
    return dominant(key, ROOT_ROWS, SEP_ROWS)


def draw_inverse_lower(key, part):
    return dominant(key, 2 * ROOT_ROWS, SEP_ROWS)


def with_ends(entries, key, least, top_value):
    longest = entries.shape.index(max(entries.shape))
    spots = []
    for shift in (0, 1):
        where = [jax.random.randint(jax.random.fold_in(key, axis), (), 0, length) for axis, length in enumerate(entries.shape)]
        where[longest] = (where[longest] + shift) % entries.shape[longest]
        spots.append(tuple(where))
    return entries.at[spots[0]].set(least).at[spots[1]].set(top_value)


def block_scale(stream_key, extent, cuts, low, high):
    def one(position, shards_of):
        steps = jax.random.uniform(jax.random.fold_in(jax.random.fold_in(stream_key, 6), position), (shards_of,), jnp.float32, low / len(cuts), high / len(cuts))
        return jnp.repeat(jnp.exp(steps), extent[position] // shards_of).reshape((-1,) + (1,) * (len(extent) - position - 1))

    gain = one(*cuts[0])
    for cut in cuts[1:]:
        gain = gain * one(*cut)
    return gain


def bell_draw(rng, shape, scale, limit, shards=(), kind=jnp.bfloat16):
    level = block_scale(rng, shape, shards, -0.22, 0.18) if shards else 1.0
    drawn = jax.random.normal(rng, shape, jnp.float32) * scale * level
    return jnp.minimum(jnp.maximum(drawn, -limit), limit).astype(kind)


def setup_inputs(seed: int = 0) -> dict:
    arg_keys = jax.random.split(jax.random.key(seed), 9)
    return {
        "right_side": bell_draw(arg_keys[0], (4 * ROOT_ROWS, RHS), 1.0, 6.0, ((0, 32),), jnp.float32),
        "inverse_root": draw_inverse_root(jax.random.fold_in(arg_keys[8], 71), 0),
        "inverse_middle": draw_inverse_middle(jax.random.fold_in(arg_keys[8], 71), 0),
        "inverse_lower": draw_inverse_lower(jax.random.fold_in(arg_keys[8], 71), 0),
        "update_middle": bell_draw(arg_keys[4], (ROOT_ROWS, MID_UPD), SEP_ROWS ** -0.5, 0.09375, ((0, 32),)),
        "update_lower": bell_draw(arg_keys[5], (2 * ROOT_ROWS, LOW_UPD), SEP_ROWS ** -0.5, 0.09375, ((0, 32),)),
        "target_middle": with_ends(jax.random.randint(arg_keys[6], (N_LEAF * N_SEP, SLOTS), 0, DEV_ROWS // BLOCK), jax.random.fold_in(arg_keys[6], 1), 0, (DEV_ROWS // BLOCK) - 1).astype(jnp.int32),
        "target_lower": with_ends(jax.random.randint(arg_keys[7], (N_LEAF * N_SEP, SLOTS), 0, 2 * DEV_ROWS // BLOCK), jax.random.fold_in(arg_keys[7], 1), 0, (2 * DEV_ROWS // BLOCK) - 1).astype(jnp.int32),
    }


def reference(right_side, inverse_root, inverse_middle, inverse_lower, update_middle, update_lower, target_middle, target_lower):
    devices = N_LEAF * N_SEP
    grouped = right_side.reshape(devices, 4 * DEV_ROWS, RHS)
    root_side = grouped[:, :DEV_ROWS].reshape(ROOT_ROWS, RHS)
    middle_side = grouped[:, DEV_ROWS:2 * DEV_ROWS].reshape(ROOT_ROWS, RHS)
    lower_side = grouped[:, 2 * DEV_ROWS:].reshape(2 * ROOT_ROWS, RHS)
    span = SLOTS * BLOCK
    middle_rows = jnp.arange(MID_UPD, dtype=jnp.int32)
    middle_targets = []
    for middle in range(2):
        owner = (middle * (devices // 2) + middle_rows // span).astype(jnp.int32)
        which = ((middle_rows // BLOCK) % SLOTS).astype(jnp.int32)
        place = target_middle[owner, which] * BLOCK + middle_rows % BLOCK
        middle_targets.append((owner * DEV_ROWS + place).astype(jnp.int32))
    lower_rows = jnp.arange(LOW_UPD, dtype=jnp.int32)
    lower_targets = []
    for lower in range(4):
        owner = (lower * (devices // 4) + lower_rows // span).astype(jnp.int32)
        which = ((lower_rows // BLOCK) % SLOTS).astype(jnp.int32)
        place = target_lower[owner, which] * BLOCK + lower_rows % BLOCK
        inside = owner * DEV_ROWS + place
        lower_targets.append(jnp.where(place < DEV_ROWS, inside, ROOT_ROWS + inside - DEV_ROWS).astype(jnp.int32))
    lower_words = lower_side.astype(jnp.bfloat16)
    accum = jnp.zeros((2 * ROOT_ROWS, RHS), jnp.float32)
    lower_values = []
    for lower in range(4):
        start = lower * SEP_ROWS
        words = lower_words[start:start + SEP_ROWS]
        lower_values.append(jnp.dot(inverse_lower[start:start + SEP_ROWS], words, preferred_element_type=jnp.float32))
        contrib = jnp.dot(update_lower[start:start + SEP_ROWS].T, words, preferred_element_type=jnp.float32)
        accum = accum.at[lower_targets[lower]].add(contrib)
    middle_words = (middle_side - accum[ROOT_ROWS:]).astype(jnp.bfloat16)
    middle_values = []
    for middle in range(2):
        start = middle * SEP_ROWS
        words = middle_words[start:start + SEP_ROWS]
        middle_values.append(jnp.dot(inverse_middle[start:start + SEP_ROWS], words, preferred_element_type=jnp.float32))
        contrib = jnp.dot(update_middle[start:start + SEP_ROWS].T, words, preferred_element_type=jnp.float32)
        accum = accum.at[middle_targets[middle]].add(contrib)
    root_words = (root_side - accum[:ROOT_ROWS]).astype(jnp.bfloat16)
    root_solution = jnp.dot(inverse_root, root_words, preferred_element_type=jnp.float32)
    root_rounded = root_solution.astype(jnp.bfloat16)
    middle_parts = []
    for middle in range(2):
        start = middle * SEP_ROWS
        picked = root_rounded[middle_targets[middle]]
        middle_parts.append(middle_values[middle] - jnp.dot(update_middle[start:start + SEP_ROWS], picked, preferred_element_type=jnp.float32))
    middle_solution = jnp.concatenate(middle_parts, axis=0)
    middle_rounded = middle_solution.astype(jnp.bfloat16)
    table = jnp.concatenate([root_rounded, middle_rounded], axis=0)
    lower_parts = []
    for lower in range(4):
        start = lower * SEP_ROWS
        picked = table[lower_targets[lower]]
        lower_parts.append(lower_values[lower] - jnp.dot(update_lower[start:start + SEP_ROWS], picked, preferred_element_type=jnp.float32))
    lower_solution = jnp.concatenate(lower_parts, axis=0)
    joined = jnp.concatenate([root_solution.reshape(devices, DEV_ROWS, RHS), middle_solution.reshape(devices, DEV_ROWS, RHS), lower_solution.reshape(devices, 2 * DEV_ROWS, RHS)], axis=1)
    return joined.reshape(4 * ROOT_ROWS, RHS)
```

```python
import jax
import jax.numpy as jnp
from jax import lax
from jax.experimental import pallas as pl
from jax.experimental.pallas import tpu as pltpu
from jax.sharding import PartitionSpec as P

BLOCK = 8


def from_partner(block, axis, distance):
    count = lax.axis_size(axis)
    route = []
    for low in range(count):
        high = low | 1 << distance
        if high != low and high < count:
            route += [(low, high), (high, low)]
    return lax.ppermute(block, axis, route)


def on_device(
    right_side,
    inverse_root,
    inverse_middle,
    inverse_lower,
    update_middle,
    update_lower,
    target_middle,
    target_lower,
):
    leaf_index = lax.axis_index("leaf")
    leaf_count = lax.axis_size("leaf")
    leaf_bits = leaf_count.bit_length() - 1
    dev_rows = inverse_root.shape[0]
    width = right_side.shape[1]
    root_side = right_side[:dev_rows]
    middle_side = right_side[dev_rows : 2 * dev_rows]
    lower_side = right_side[2 * dev_rows :]

    def collect(piece, depth_bits):
        panel = lax.all_gather(piece, "sep", axis=0, tiled=True)
        for bit_index in range(depth_bits):
            partner = from_partner(panel, "leaf", bit_index)
            upper = leaf_index >> bit_index & 1 == 1
            first = jnp.where(upper, partner, panel)
            second = jnp.where(upper, panel, partner)
            panel = jnp.concatenate([first, second], axis=0)
        return panel

    def apply_inverse(inverse, words, depth_bits):
        panel = collect(words, depth_bits)
        return jnp.dot(inverse, panel, preferred_element_type=jnp.float32)

    def halve_whole(current, depth_bits):
        for bit_index in reversed(range(depth_bits)):
            half = current.shape[0] // 2
            upper = leaf_index >> bit_index & 1 == 1
            keep = jnp.where(upper, current[half:], current[:half])
            give = jnp.where(upper, current[:half], current[half:])
            current = keep + from_partner(give, "leaf", bit_index)
        return current

    def reduce_slots(partial_value, depth_bits):
        current = halve_whole(partial_value, depth_bits)
        return lax.psum_scatter(current, "sep", scatter_dimension=0, tiled=True)

    def selector(targets, blocks):
        return (jnp.arange(blocks, dtype=jnp.int32)[:, None] == targets[0][None, :]).astype(
            jnp.float32
        )

    def place_slots(summed, targets, blocks):
        onehot = selector(targets, blocks)
        flat = summed.reshape(targets.shape[1], BLOCK * width)
        placed = jnp.dot(onehot, flat, precision=lax.Precision.HIGHEST)
        return placed.reshape(blocks * BLOCK, width)

    def pick_slots(table, targets, blocks):
        onehot = selector(targets, blocks)
        flat = table.astype(jnp.float32).reshape(blocks, BLOCK * width)
        picked = jnp.dot(onehot.T, flat, precision=lax.Precision.HIGHEST)
        return picked.reshape(targets.shape[1] * BLOCK, width).astype(jnp.bfloat16)

    contract_rows = (((0,), (0,)), ((), ()))
    lower_blocks = 2 * dev_rows // BLOCK
    middle_blocks = dev_rows // BLOCK
    lower_words = lower_side.astype(jnp.bfloat16)
    lower_values = apply_inverse(inverse_lower, lower_words, leaf_bits - 2)
    lower_partial = lax.dot_general(
        update_lower, lower_words, contract_rows, preferred_element_type=jnp.float32
    )
    lower_accum = place_slots(
        reduce_slots(lower_partial, leaf_bits - 2), target_lower, lower_blocks
    )
    middle_words = (middle_side - lower_accum[dev_rows:]).astype(jnp.bfloat16)
    middle_values = apply_inverse(inverse_middle, middle_words, leaf_bits - 1)
    middle_partial = lax.dot_general(
        update_middle, middle_words, contract_rows, preferred_element_type=jnp.float32
    )
    middle_accum = place_slots(
        reduce_slots(middle_partial, leaf_bits - 1), target_middle, middle_blocks
    )
    root_words = (root_side - (lower_accum[:dev_rows] + middle_accum)).astype(jnp.bfloat16)
    root_solution = apply_inverse(inverse_root, root_words, leaf_bits)
    root_rounded = root_solution.astype(jnp.bfloat16)
    middle_slots = collect(pick_slots(root_rounded, target_middle, middle_blocks), leaf_bits - 1)
    middle_solution = middle_values - jnp.dot(
        update_middle, middle_slots, preferred_element_type=jnp.float32
    )
    middle_rounded = middle_solution.astype(jnp.bfloat16)
    table = jnp.concatenate([root_rounded, middle_rounded], axis=0)
    lower_slots = collect(pick_slots(table, target_lower, lower_blocks), leaf_bits - 2)
    lower_solution = lower_values - jnp.dot(
        update_lower, lower_slots, preferred_element_type=jnp.float32
    )
    return jnp.concatenate([root_solution, middle_solution, lower_solution], axis=0)


PLANE = 8
PAIR = 16
PLANES = 4
N_BULK = 8
MESH = pl.DeviceIdType.MESH


def fused_kernel(
    side_hbm, root_hbm, middle_hbm, lower_hbm, up_mid_hbm, up_low_hbm, target_mid, target_low, out_hbm,
    side, inv_root, inv_mid, inv_low, up_mid, up_low, low_panel, mid_panel, root_panel,
    low_part, mid_part, low_in, mid_in, low_slots, mid_slots, xs,
    load_sem, out_sem, small_send, small_recv, bulk_send, bulk_recv, z_send, z_recv,
):
    rows = root_hbm.shape[0]
    plane_cols = PLANE * rows
    leaf, sep = lax.axis_index("leaf"), lax.axis_index("sep")
    z, x, y, c = leaf // 2, leaf % 2, sep // 2, sep % 2
    z1, z2, z3 = z + 1 - 2 * (z % 2), (z + 2) % PLANES, PLANES - 1 - z
    in_plane = x * 4 + sep
    in_pair = (leaf % 4) * 4 + sep

    def plane_peer(step):
        peer = (in_plane + step) % PLANE
        return peer, (z * 2 + peer // 4, peer % 4)

    def pair_peer(step):
        peer = (in_pair + step) % PAIR
        return peer, (leaf // 4 * 4 + peer // 4, peer % 4)

    x_peer = (z * 2 + 1 - x, sep)
    y_peer = (leaf, (1 - y) * 2 + c)
    sibling = (leaf, y * 2 + 1 - c)

    barrier = pltpu.get_barrier_semaphore()
    for step in range(1, PAIR):
        pl.semaphore_signal(barrier, inc=1, device_id=pair_peer(step)[1], device_id_type=MESH)
    for far in (z2, z3):
        pl.semaphore_signal(barrier, inc=1, device_id=(far * 2 + x, sep), device_id_type=MESH)

    loads = [
        pltpu.make_async_copy(side_hbm.at[pl.ds(2 * rows, 2 * rows)], side.at[pl.ds(2 * rows, 2 * rows)], load_sem.at[0]),
        pltpu.make_async_copy(up_low_hbm, up_low, load_sem.at[1]),
        pltpu.make_async_copy(side_hbm.at[pl.ds(0, 2 * rows)], side.at[pl.ds(0, 2 * rows)], load_sem.at[2]),
        pltpu.make_async_copy(up_mid_hbm, up_mid, load_sem.at[3]),
        pltpu.make_async_copy(lower_hbm, inv_low, load_sem.at[4]),
    ]
    for half in range(2):
        loads.append(
            pltpu.make_async_copy(
                middle_hbm.at[:, pl.ds(half * plane_cols, plane_cols)], inv_mid.at[half], load_sem.at[5 + half]
            )
        )
    for plane in range(PLANES):
        loads.append(
            pltpu.make_async_copy(
                root_hbm.at[:, pl.ds(plane * plane_cols, plane_cols)], inv_root.at[plane], load_sem.at[7 + plane]
            )
        )
    for load in loads:
        load.start()

    started = []

    def send(source, target, send_sem, recv_sem, device):
        copy = pltpu.make_async_remote_copy(
            src_ref=source, dst_ref=target, send_sem=send_sem, recv_sem=recv_sem,
            device_id=device, device_id_type=MESH,
        )
        copy.start()
        started.append(copy)

    def arrived(ref, recv_sem):
        pltpu.make_async_remote_copy(
            src_ref=ref, dst_ref=ref, send_sem=small_send.at[0], recv_sem=recv_sem,
            device_id=sibling, device_id_type=MESH,
        ).wait_recv()

    class Gather:
        def __init__(self, panel, size, first, index):
            self.panel, self.size, self.first, self.index = panel, size, first, index

        def ref(self, px, py, pc, start=0, size=None):
            where = (self.first + px * 4 + py * 2 + pc) * self.size + start
            return self.panel.at[pl.ds(pl.multiple_of(where, 64), size or self.size)]

        def sems(self, kind):
            place = self.index * N_BULK + kind
            return bulk_send.at[place], bulk_recv.at[place]

        def copy(self, ref, kind, device):
            send(ref, ref, *self.sems(kind), device)

        def wait(self, ref, kind):
            arrived(ref, self.sems(kind)[1])

        def own(self):
            ref = self.ref(x, y, c)
            self.copy(ref, 0, x_peer)
            self.copy(ref, 1, y_peer)
            self.copy(ref, 2, sibling)

        def pass_on(self):
            half = self.size // 2
            ref = self.ref(1 - x, y, c)
            self.wait(ref, 0)
            self.copy(self.ref(1 - x, y, c, 0, half), 3, y_peer)
            self.copy(ref, 5, sibling)
            ref = self.ref(x, 1 - y, c)
            self.wait(ref, 1)
            self.copy(self.ref(x, 1 - y, c, half, half), 4, x_peer)
            self.copy(ref, 6, sibling)

        def pass_far(self):
            half = self.size // 2
            self.wait(self.ref(1 - x, 1 - y, c, 0, half), 3)
            self.wait(self.ref(1 - x, 1 - y, c, half, half), 4)
            self.copy(self.ref(1 - x, 1 - y, c), 7, sibling)

        def finish(self):
            self.wait(self.ref(x, y, 1 - c), 2)
            self.wait(self.ref(1 - x, y, 1 - c), 5)
            self.wait(self.ref(x, 1 - y, 1 - c), 6)
            self.wait(self.ref(1 - x, 1 - y, 1 - c), 7)

    low = Gather(low_panel, 2 * rows, 0, 0)
    mids = [Gather(mid_panel, rows, (zz % 2) * PLANE, 1 + i) for i, zz in enumerate((z, z1))]
    roots = [Gather(root_panel, rows, zz * PLANE, 3 + i) for i, zz in enumerate((z, z1, z2, z3))]

    contract = (((0,), (0,)), ((), ()))

    def spread(block, position):
        wide = jnp.broadcast_to(block[None], (rows // BLOCK,) + block.shape).reshape(rows, block.shape[1])
        place = lax.broadcasted_iota(jnp.int32, wide.shape, 0) // BLOCK
        return jnp.where(place == position, wide, 0.0)

    loads[0].wait()
    loads[1].wait()
    low_words = side[2 * rows :, :].astype(jnp.bfloat16)
    low.ref(x, y, c)[...] = low_words
    low_part[...] = lax.dot_general(up_low[...], low_words, contract, preferred_element_type=jnp.float32)
    pl.semaphore_wait(barrier, PAIR - 1 + 2)

    def exchange(part, landing, count, peer_of, base):
        for step in reversed(range(1, count)):
            peer, device = peer_of(step)
            source = part.at[pl.ds(pl.multiple_of(peer * BLOCK, BLOCK), BLOCK)]
            send(source, landing.at[step], small_send.at[base + step], small_recv.at[base + step], device)

    def collected(part, landing, count, mine, base):
        total = part[pl.ds(pl.multiple_of(mine * BLOCK, BLOCK), BLOCK), :]
        for step in range(1, count):
            arrived(landing.at[step], small_recv.at[base + step])
        for step in range(1, count):
            total = total + landing[step]
        return total

    exchange(low_part, low_in, PLANE, plane_peer, 0)
    low.own()
    loads[2].wait()
    loads[3].wait()
    low_sum = collected(low_part, low_in, PLANE, in_plane, 0)

    low_target = target_low[0, 0]
    mid_target = target_mid[0, 0]
    mid_words = (side[rows : 2 * rows, :] - spread(low_sum, low_target - rows // BLOCK)).astype(jnp.bfloat16)
    mids[0].ref(x, y, c)[...] = mid_words
    mid_part[...] = lax.dot_general(up_mid[...], mid_words, contract, preferred_element_type=jnp.float32)
    exchange(mid_part, mid_in, PAIR, pair_peer, PLANE)
    ref = mids[0].ref(x, y, c)
    send(ref, ref, z_send.at[0], z_recv.at[0], (z1 * 2 + x, sep))
    mids[0].own()
    low.pass_on()
    mid_sum = collected(mid_part, mid_in, PAIR, in_pair, PLANE)

    root_words = (side[:rows, :] - (spread(low_sum, low_target) + spread(mid_sum, mid_target))).astype(jnp.bfloat16)
    ref = roots[0].ref(x, y, c)
    ref[...] = root_words
    for i, zz in ((3, z3), (2, z2), (1, z1)):
        send(ref, ref, z_send.at[i], z_recv.at[i], (zz * 2 + x, sep))
    roots[0].own()

    arrived(mids[1].ref(x, y, c), z_recv.at[0])
    mids[1].own()
    low.pass_far()
    mids[0].pass_on()
    arrived(roots[1].ref(x, y, c), z_recv.at[1])
    roots[1].own()
    low.finish()
    loads[4].wait()

    chunk = 1024
    xs[2 * rows :, :] = jnp.zeros((2 * rows, xs.shape[1]), jnp.float32)

    def low_step(first, last):
        @pl.loop(first, last)
        def _(i):
            start = pl.multiple_of(i * chunk, chunk)
            xs[2 * rows :, :] += jnp.dot(
                inv_low[:, pl.ds(start, chunk)], low_panel[pl.ds(start, chunk), :],
                preferred_element_type=jnp.float32,
            )

    chunks = low_panel.shape[0] // chunk
    low_step(0, chunks // 2)
    mids[1].pass_on()
    mids[0].pass_far()
    arrived(roots[2].ref(x, y, c), z_recv.at[2])
    roots[2].own()
    roots[0].pass_on()
    arrived(roots[3].ref(x, y, c), z_recv.at[3])
    roots[3].own()
    low_step(chunks // 2, chunks)
    mids[1].pass_far()
    roots[1].pass_on()
    roots[0].pass_far()
    mids[0].finish()
    mids[1].finish()
    loads[5].wait()
    loads[6].wait()
    xs[rows : 2 * rows, :] = jnp.zeros((rows, xs.shape[1]), jnp.float32)
    xs[:rows, :] = jnp.zeros((rows, xs.shape[1]), jnp.float32)

    def mid_step(half):
        start = half * plane_cols
        xs[rows : 2 * rows, :] += jnp.dot(
            inv_mid[half], mid_panel[start : start + plane_cols, :], preferred_element_type=jnp.float32
        )

    def root_step(gather, plane):
        start = pl.multiple_of(plane * plane_cols, plane_cols)
        xs[:rows, :] += jnp.dot(
            inv_root[plane], root_panel[pl.ds(start, plane_cols), :], preferred_element_type=jnp.float32
        )

    mid_step(0)
    roots[2].pass_on()
    roots[1].pass_far()
    mid_step(1)
    roots[3].pass_on()
    for plane in range(PLANES):
        loads[7 + plane].wait()
    roots[0].finish()
    root_step(roots[0], z)
    roots[2].pass_far()
    roots[1].finish()
    root_step(roots[1], z1)
    roots[3].pass_far()
    roots[2].finish()
    root_step(roots[2], z2)
    roots[3].finish()
    root_step(roots[3], z3)

    def share(slots, position, count, mine, peer_of, base):
        rows_of = pl.ds(pl.multiple_of(mine * BLOCK, BLOCK), BLOCK)
        table = xs[: 2 * rows, :].reshape(2 * rows // BLOCK, BLOCK, xs.shape[1])
        place = lax.broadcasted_iota(jnp.int32, table.shape, 0)
        slots[rows_of, :] = jnp.sum(jnp.where(place == position, table, 0.0), axis=0)
        for step in reversed(range(1, count)):
            send(slots.at[rows_of], slots.at[rows_of], small_send.at[base + step], small_recv.at[base + step], peer_of(step)[1])

    def shared(slots, count, mine, base):
        for step in range(1, count):
            source = (mine + count - step) % count
            arrived(slots.at[pl.ds(pl.multiple_of(source * BLOCK, BLOCK), BLOCK)], small_recv.at[base + step])
        return slots[...].astype(jnp.bfloat16)

    def store(piece, start, size):
        copy = pltpu.make_async_copy(xs.at[pl.ds(start, size)], out_hbm.at[pl.ds(start, size)], out_sem.at[piece])
        copy.start()
        return copy

    share(mid_slots, mid_target, PAIR, in_pair, pair_peer, PLANE + PAIR)
    stores = [store(0, 0, rows)]
    slots = shared(mid_slots, PAIR, in_pair, PLANE + PAIR)
    xs[rows : 2 * rows, :] -= jnp.dot(up_mid[...], slots, preferred_element_type=jnp.float32)
    share(low_slots, low_target, PLANE, in_plane, plane_peer, PLANE + 2 * PAIR)
    stores.append(store(1, rows, rows))
    slots = shared(low_slots, PLANE, in_plane, PLANE + 2 * PAIR)
    xs[2 * rows :, :] -= jnp.dot(up_low[...], slots, preferred_element_type=jnp.float32)
    stores.append(store(2, 2 * rows, 2 * rows))
    for copy in started:
        copy.wait_send()
    for copy in stores:
        copy.wait()


def on_device_fused(
    right_side, inverse_root, inverse_middle, inverse_lower, update_middle, update_lower, target_middle, target_lower
):
    rows = inverse_root.shape[0]
    width = right_side.shape[1]
    plane_cols = PLANE * rows
    groups = 1 + 2 + PLANES
    small = 2 * PLANE + 2 * PAIR
    half, full = jnp.bfloat16, jnp.float32
    dma = pltpu.SemaphoreType.DMA
    hbm = pl.BlockSpec(memory_space=pl.ANY)
    scalar = pl.BlockSpec(memory_space=pltpu.SMEM)
    return pl.pallas_call(
        fused_kernel,
        out_shape=jax.ShapeDtypeStruct(right_side.shape, full),
        in_specs=[hbm] * 6 + [scalar] * 2,
        out_specs=hbm,
        scratch_shapes=[
            pltpu.VMEM(right_side.shape, full),
            pltpu.VMEM((PLANES, rows, plane_cols), half),
            pltpu.VMEM((2, rows, plane_cols), half),
            pltpu.VMEM(inverse_lower.shape, half),
            pltpu.VMEM(update_middle.shape, half),
            pltpu.VMEM(update_lower.shape, half),
            pltpu.VMEM((2 * rows * PLANE, width), half),
            pltpu.VMEM((rows * PAIR, width), half),
            pltpu.VMEM((rows * PLANE * PLANES, width), half),
            pltpu.VMEM((PLANE * BLOCK, width), full),
            pltpu.VMEM((PAIR * BLOCK, width), full),
            pltpu.VMEM((PLANE, BLOCK, width), full),
            pltpu.VMEM((PAIR, BLOCK, width), full),
            pltpu.VMEM((PLANE * BLOCK, width), full),
            pltpu.VMEM((PAIR * BLOCK, width), full),
            pltpu.VMEM(right_side.shape, full),
            dma((7 + PLANES,)),
            dma((3,)),
            dma((small,)),
            dma((small,)),
            dma((groups * N_BULK,)),
            dma((groups * N_BULK,)),
            dma((PLANES,)),
            dma((PLANES,)),
        ],
        compiler_params=pltpu.CompilerParams(
            collective_id=0, has_side_effects=True, vmem_limit_bytes=40 * 1024 * 1024
        ),
    )(right_side, inverse_root, inverse_middle, inverse_lower, update_middle, update_lower, target_middle, target_lower)


def solution(mesh):
    in_specs = (
        P(("leaf", "sep"), None),
        P(("leaf", "sep"), None),
        P(("leaf", "sep"), None),
        P(("leaf", "sep"), None),
        P(("leaf", "sep"), None),
        P(("leaf", "sep"), None),
        P(("leaf", "sep"), None),
        P(("leaf", "sep"), None),
    )
    out_specs = P(("leaf", "sep"), None)
    fits = dict(mesh.shape) == {"leaf": 8, "sep": 4}
    return jax.shard_map(
        on_device_fused if fits else on_device, mesh=mesh, in_specs=in_specs, out_specs=out_specs, check_vma=False
    )
```

```python
import jax
import jax.numpy as jnp
from jax import lax
from jax.experimental import pallas as pl
from jax.experimental.pallas import tpu as pltpu
from jax.sharding import PartitionSpec as P

BLOCK = 8


def from_partner(block, axis, distance):
    count = lax.axis_size(axis)
    route = []
    for low in range(count):
        high = low | 1 << distance
        if high != low and high < count:
            route += [(low, high), (high, low)]
    return lax.ppermute(block, axis, route)


def on_device(
    right_side,
    inverse_root,
    inverse_middle,
    inverse_lower,
    update_middle,
    update_lower,
    target_middle,
    target_lower,
):
    leaf_index = lax.axis_index("leaf")
    leaf_count = lax.axis_size("leaf")
    leaf_bits = leaf_count.bit_length() - 1
    dev_rows = inverse_root.shape[0]
    width = right_side.shape[1]
    root_side = right_side[:dev_rows]
    middle_side = right_side[dev_rows : 2 * dev_rows]
    lower_side = right_side[2 * dev_rows :]

    def collect(piece, depth_bits):
        panel = lax.all_gather(piece, "sep", axis=0, tiled=True)
        for bit_index in range(depth_bits):
            partner = from_partner(panel, "leaf", bit_index)
            upper = leaf_index >> bit_index & 1 == 1
            first = jnp.where(upper, partner, panel)
            second = jnp.where(upper, panel, partner)
            panel = jnp.concatenate([first, second], axis=0)
        return panel

    def apply_inverse(inverse, words, depth_bits):
        panel = collect(words, depth_bits)
        return jnp.dot(inverse, panel, preferred_element_type=jnp.float32)

    def halve_whole(current, depth_bits):
        for bit_index in reversed(range(depth_bits)):
            half = current.shape[0] // 2
            upper = leaf_index >> bit_index & 1 == 1
            keep = jnp.where(upper, current[half:], current[:half])
            give = jnp.where(upper, current[:half], current[half:])
            current = keep + from_partner(give, "leaf", bit_index)
        return current

    def reduce_slots(partial_value, depth_bits):
        current = halve_whole(partial_value, depth_bits)
        return lax.psum_scatter(current, "sep", scatter_dimension=0, tiled=True)

    def selector(targets, blocks):
        return (jnp.arange(blocks, dtype=jnp.int32)[:, None] == targets[0][None, :]).astype(
            jnp.float32
        )

    def place_slots(summed, targets, blocks):
        onehot = selector(targets, blocks)
        flat = summed.reshape(targets.shape[1], BLOCK * width)
        placed = jnp.dot(onehot, flat, precision=lax.Precision.HIGHEST)
        return placed.reshape(blocks * BLOCK, width)

    def pick_slots(table, targets, blocks):
        onehot = selector(targets, blocks)
        flat = table.astype(jnp.float32).reshape(blocks, BLOCK * width)
        picked = jnp.dot(onehot.T, flat, precision=lax.Precision.HIGHEST)
        return picked.reshape(targets.shape[1] * BLOCK, width).astype(jnp.bfloat16)

    contract_rows = (((0,), (0,)), ((), ()))
    lower_blocks = 2 * dev_rows // BLOCK
    middle_blocks = dev_rows // BLOCK
    lower_words = lower_side.astype(jnp.bfloat16)
    lower_values = apply_inverse(inverse_lower, lower_words, leaf_bits - 2)
    lower_partial = lax.dot_general(
        update_lower, lower_words, contract_rows, preferred_element_type=jnp.float32
    )
    lower_accum = place_slots(
        reduce_slots(lower_partial, leaf_bits - 2), target_lower, lower_blocks
    )
    middle_words = (middle_side - lower_accum[dev_rows:]).astype(jnp.bfloat16)
    middle_values = apply_inverse(inverse_middle, middle_words, leaf_bits - 1)
    middle_partial = lax.dot_general(
        update_middle, middle_words, contract_rows, preferred_element_type=jnp.float32
    )
    middle_accum = place_slots(
        reduce_slots(middle_partial, leaf_bits - 1), target_middle, middle_blocks
    )
    root_words = (root_side - (lower_accum[:dev_rows] + middle_accum)).astype(jnp.bfloat16)
    root_solution = apply_inverse(inverse_root, root_words, leaf_bits)
    root_rounded = root_solution.astype(jnp.bfloat16)
    middle_slots = collect(pick_slots(root_rounded, target_middle, middle_blocks), leaf_bits - 1)
    middle_solution = middle_values - jnp.dot(
        update_middle, middle_slots, preferred_element_type=jnp.float32
    )
    middle_rounded = middle_solution.astype(jnp.bfloat16)
    table = jnp.concatenate([root_rounded, middle_rounded], axis=0)
    lower_slots = collect(pick_slots(table, target_lower, lower_blocks), leaf_bits - 2)
    lower_solution = lower_values - jnp.dot(
        update_lower, lower_slots, preferred_element_type=jnp.float32
    )
    return jnp.concatenate([root_solution, middle_solution, lower_solution], axis=0)


PLANE = 8
PAIR = 16
PLANES = 4
N_BULK = 8
MESH = pl.DeviceIdType.MESH


def fused_kernel(
    side_hbm, root_hbm, middle_hbm, lower_hbm, up_mid_hbm, up_low_hbm, target_mid, target_low, out_hbm,
    side, inv_root, inv_mid, inv_low, up_mid, up_low, low_panel, mid_panel, root_panel,
    low_part, mid_part, low_in, mid_in, low_slots, mid_slots, xs,
    load_sem, out_sem, small_send, small_recv, bulk_send, bulk_recv, z_send, z_recv,
):
    rows = root_hbm.shape[0]
    plane_cols = PLANE * rows
    leaf, sep = lax.axis_index("leaf"), lax.axis_index("sep")
    z, x, y, c = leaf // 2, leaf % 2, sep // 2, sep % 2
    z1, z2, z3 = z + 1 - 2 * (z % 2), (z + 2) % PLANES, PLANES - 1 - z
    in_plane = x * 4 + sep
    in_pair = (leaf % 4) * 4 + sep

    def plane_peer(step):
        peer = (in_plane + step) % PLANE
        return peer, (z * 2 + peer // 4, peer % 4)

    def pair_peer(step):
        peer = (in_pair + step) % PAIR
        return peer, (leaf // 4 * 4 + peer // 4, peer % 4)

    x_peer = (z * 2 + 1 - x, sep)
    y_peer = (leaf, (1 - y) * 2 + c)
    sibling = (leaf, y * 2 + 1 - c)

    barrier = pltpu.get_barrier_semaphore()
    for step in range(1, PAIR):
        pl.semaphore_signal(barrier, inc=1, device_id=pair_peer(step)[1], device_id_type=MESH)
    for far in (z2, z3):
        pl.semaphore_signal(barrier, inc=1, device_id=(far * 2 + x, sep), device_id_type=MESH)

    loads = [
        pltpu.make_async_copy(side_hbm.at[pl.ds(2 * rows, 2 * rows)], side.at[pl.ds(2 * rows, 2 * rows)], load_sem.at[0]),
        pltpu.make_async_copy(up_low_hbm, up_low, load_sem.at[1]),
        pltpu.make_async_copy(side_hbm.at[pl.ds(0, 2 * rows)], side.at[pl.ds(0, 2 * rows)], load_sem.at[2]),
        pltpu.make_async_copy(up_mid_hbm, up_mid, load_sem.at[3]),
        pltpu.make_async_copy(lower_hbm, inv_low, load_sem.at[4]),
    ]
    for half in range(2):
        loads.append(
            pltpu.make_async_copy(
                middle_hbm.at[:, pl.ds(half * plane_cols, plane_cols)], inv_mid.at[half], load_sem.at[5 + half]
            )
        )
    for plane in range(PLANES):
        loads.append(
            pltpu.make_async_copy(
                root_hbm.at[:, pl.ds(plane * plane_cols, plane_cols)], inv_root.at[plane], load_sem.at[7 + plane]
            )
        )
    for load in loads:
        load.start()

    started = []

    def send(source, target, send_sem, recv_sem, device):
        copy = pltpu.make_async_remote_copy(
            src_ref=source, dst_ref=target, send_sem=send_sem, recv_sem=recv_sem,
            device_id=device, device_id_type=MESH,
        )
        copy.start()
        started.append(copy)

    def arrived(ref, recv_sem):
        pltpu.make_async_remote_copy(
            src_ref=ref, dst_ref=ref, send_sem=small_send.at[0], recv_sem=recv_sem,
            device_id=sibling, device_id_type=MESH,
        ).wait_recv()

    class Gather:
        def __init__(self, panel, size, first, index):
            self.panel, self.size, self.first, self.index = panel, size, first, index

        def ref(self, px, py, pc, start=0, size=None):
            where = (self.first + px * 4 + py * 2 + pc) * self.size + start
            return self.panel.at[pl.ds(pl.multiple_of(where, 64), size or self.size)]

        def sems(self, kind):
            place = self.index * N_BULK + kind
            return bulk_send.at[place], bulk_recv.at[place]

        def copy(self, ref, kind, device):
            send(ref, ref, *self.sems(kind), device)

        def wait(self, ref, kind):
            arrived(ref, self.sems(kind)[1])

        def own(self):
            ref = self.ref(x, y, c)
            self.copy(ref, 0, x_peer)
            self.copy(ref, 1, y_peer)
            self.copy(ref, 2, sibling)

        def pass_on(self):
            half = self.size // 2
            ref = self.ref(1 - x, y, c)
            self.wait(ref, 0)
            self.copy(self.ref(1 - x, y, c, 0, half), 3, y_peer)
            self.copy(ref, 5, sibling)
            ref = self.ref(x, 1 - y, c)
            self.wait(ref, 1)
            self.copy(self.ref(x, 1 - y, c, half, half), 4, x_peer)
            self.copy(ref, 6, sibling)

        def pass_far(self):
            half = self.size // 2
            self.wait(self.ref(1 - x, 1 - y, c, 0, half), 3)
            self.wait(self.ref(1 - x, 1 - y, c, half, half), 4)
            self.copy(self.ref(1 - x, 1 - y, c), 7, sibling)

        def finish(self):
            self.wait(self.ref(x, y, 1 - c), 2)
            self.wait(self.ref(1 - x, y, 1 - c), 5)
            self.wait(self.ref(x, 1 - y, 1 - c), 6)
            self.wait(self.ref(1 - x, 1 - y, 1 - c), 7)

    low = Gather(low_panel, 2 * rows, 0, 0)
    mids = [Gather(mid_panel, rows, (zz % 2) * PLANE, 1 + i) for i, zz in enumerate((z, z1))]
    roots = [Gather(root_panel, rows, zz * PLANE, 3 + i) for i, zz in enumerate((z, z1, z2, z3))]

    contract = (((0,), (0,)), ((), ()))

    def spread(block, position):
        wide = jnp.broadcast_to(block[None], (rows // BLOCK,) + block.shape).reshape(rows, block.shape[1])
        place = lax.broadcasted_iota(jnp.int32, wide.shape, 0) // BLOCK
        return jnp.where(place == position, wide, 0.0)

    loads[0].wait()
    loads[1].wait()
    low_words = side[2 * rows :, :].astype(jnp.bfloat16)
    low.ref(x, y, c)[...] = low_words
    low_part[...] = jnp.dot(up_low[...], low_words, preferred_element_type=jnp.float32)
    pl.semaphore_wait(barrier, PAIR - 1 + 2)

    def exchange(part, landing, count, peer_of, base):
        for step in reversed(range(1, count)):
            peer, device = peer_of(step)
            source = part.at[pl.ds(pl.multiple_of(peer * BLOCK, BLOCK), BLOCK)]
            send(source, landing.at[step], small_send.at[base + step], small_recv.at[base + step], device)

    def collected(part, landing, count, mine, base):
        total = part[pl.ds(pl.multiple_of(mine * BLOCK, BLOCK), BLOCK), :]
        for step in range(1, count):
            arrived(landing.at[step], small_recv.at[base + step])
        for step in range(1, count):
            total = total + landing[step]
        return total

    exchange(low_part, low_in, PLANE, plane_peer, 0)
    low.own()
    loads[2].wait()
    loads[3].wait()
    low_sum = collected(low_part, low_in, PLANE, in_plane, 0)

    low_target = target_low[0, 0]
    mid_target = target_mid[0, 0]
    mid_words = (side[rows : 2 * rows, :] - spread(low_sum, low_target - rows // BLOCK)).astype(jnp.bfloat16)
    mids[0].ref(x, y, c)[...] = mid_words
    mid_part[...] = lax.dot_general(up_mid[...], mid_words, contract, preferred_element_type=jnp.float32)
    exchange(mid_part, mid_in, PAIR, pair_peer, PLANE)
    ref = mids[0].ref(x, y, c)
    send(ref, ref, z_send.at[0], z_recv.at[0], (z1 * 2 + x, sep))
    mids[0].own()
    low.pass_on()
    mid_sum = collected(mid_part, mid_in, PAIR, in_pair, PLANE)

    root_words = (side[:rows, :] - (spread(low_sum, low_target) + spread(mid_sum, mid_target))).astype(jnp.bfloat16)
    ref = roots[0].ref(x, y, c)
    ref[...] = root_words
    for i, zz in ((3, z3), (2, z2), (1, z1)):
        send(ref, ref, z_send.at[i], z_recv.at[i], (zz * 2 + x, sep))
    roots[0].own()

    arrived(mids[1].ref(x, y, c), z_recv.at[0])
    mids[1].own()
    low.pass_far()
    mids[0].pass_on()
    arrived(roots[1].ref(x, y, c), z_recv.at[1])
    roots[1].own()
    low.finish()
    loads[4].wait()

    chunk = 1024
    xs[2 * rows :, :] = jnp.zeros((2 * rows, xs.shape[1]), jnp.float32)

    def low_step(first, last):
        @pl.loop(first, last)
        def _(i):
            start = pl.multiple_of(i * chunk, chunk)
            xs[2 * rows :, :] += jnp.dot(
                inv_low[:, pl.ds(start, chunk)], low_panel[pl.ds(start, chunk), :],
                preferred_element_type=jnp.float32,
            )

    chunks = low_panel.shape[0] // chunk
    low_step(0, chunks // 2)
    mids[1].pass_on()
    mids[0].pass_far()
    arrived(roots[2].ref(x, y, c), z_recv.at[2])
    roots[2].own()
    roots[0].pass_on()
    arrived(roots[3].ref(x, y, c), z_recv.at[3])
    roots[3].own()
    low_step(chunks // 2, chunks)
    mids[1].pass_far()
    roots[1].pass_on()
    roots[0].pass_far()
    mids[0].finish()
    mids[1].finish()
    loads[5].wait()
    loads[6].wait()
    xs[rows : 2 * rows, :] = jnp.zeros((rows, xs.shape[1]), jnp.float32)
    xs[:rows, :] = jnp.zeros((rows, xs.shape[1]), jnp.float32)

    def mid_step(half):
        start = half * plane_cols
        xs[rows : 2 * rows, :] += jnp.dot(
            inv_mid[half], mid_panel[start : start + plane_cols, :], preferred_element_type=jnp.float32
        )

    def root_step(gather, plane):
        start = pl.multiple_of(plane * plane_cols, plane_cols)
        xs[:rows, :] += jnp.dot(
            inv_root[plane], root_panel[pl.ds(start, plane_cols), :], preferred_element_type=jnp.float32
        )

    mid_step(0)
    roots[2].pass_on()
    roots[1].pass_far()
    mid_step(1)
    roots[3].pass_on()
    for plane in range(PLANES):
        loads[7 + plane].wait()
    roots[0].finish()
    root_step(roots[0], z)
    roots[2].pass_far()
    roots[1].finish()
    root_step(roots[1], z1)
    roots[3].pass_far()
    roots[2].finish()
    root_step(roots[2], z2)
    roots[3].finish()
    root_step(roots[3], z3)

    def share(slots, position, count, mine, peer_of, base):
        rows_of = pl.ds(pl.multiple_of(mine * BLOCK, BLOCK), BLOCK)
        table = xs[: 2 * rows, :].reshape(2 * rows // BLOCK, BLOCK, xs.shape[1])
        place = lax.broadcasted_iota(jnp.int32, table.shape, 0)
        slots[rows_of, :] = jnp.sum(jnp.where(place == position, table, 0.0), axis=0)
        for step in reversed(range(1, count)):
            send(slots.at[rows_of], slots.at[rows_of], small_send.at[base + step], small_recv.at[base + step], peer_of(step)[1])

    def shared(slots, count, mine, base):
        for step in range(1, count):
            source = (mine + count - step) % count
            arrived(slots.at[pl.ds(pl.multiple_of(source * BLOCK, BLOCK), BLOCK)], small_recv.at[base + step])
        return slots[...].astype(jnp.bfloat16)

    def store(piece, start, size):
        copy = pltpu.make_async_copy(xs.at[pl.ds(start, size)], out_hbm.at[pl.ds(start, size)], out_sem.at[piece])
        copy.start()
        return copy

    share(mid_slots, mid_target, PAIR, in_pair, pair_peer, PLANE + PAIR)
    stores = [store(0, 0, rows)]
    slots = shared(mid_slots, PAIR, in_pair, PLANE + PAIR)
    xs[rows : 2 * rows, :] -= jnp.dot(up_mid[...], slots, preferred_element_type=jnp.float32)
    share(low_slots, low_target, PLANE, in_plane, plane_peer, PLANE + 2 * PAIR)
    stores.append(store(1, rows, rows))
    slots = shared(low_slots, PLANE, in_plane, PLANE + 2 * PAIR)
    xs[2 * rows :, :] -= lax.dot_general(up_low[...], slots, contract, preferred_element_type=jnp.float32)
    stores.append(store(2, 2 * rows, 2 * rows))
    for copy in started:
        copy.wait_send()
    for copy in stores:
        copy.wait()


def on_device_fused(
    right_side, inverse_root, inverse_middle, inverse_lower, update_middle, update_lower, target_middle, target_lower
):
    rows = inverse_root.shape[0]
    width = right_side.shape[1]
    plane_cols = PLANE * rows
    groups = 1 + 2 + PLANES
    small = 2 * PLANE + 2 * PAIR
    half, full = jnp.bfloat16, jnp.float32
    dma = pltpu.SemaphoreType.DMA
    hbm = pl.BlockSpec(memory_space=pltpu.HBM)
    scalar = pl.BlockSpec(memory_space=pltpu.SMEM)
    return pl.pallas_call(
        fused_kernel,
        out_shape=jax.ShapeDtypeStruct(right_side.shape, full),
        in_specs=[hbm] * 6 + [scalar] * 2,
        out_specs=hbm,
        scratch_shapes=[
            pltpu.VMEM(right_side.shape, full),
            pltpu.VMEM((PLANES, rows, plane_cols), half),
            pltpu.VMEM((2, rows, plane_cols), half),
            pltpu.VMEM(inverse_lower.shape, half),
            pltpu.VMEM(update_middle.shape, half),
            pltpu.VMEM(update_lower.shape[::-1], half),
            pltpu.VMEM((2 * rows * PLANE, width), half),
            pltpu.VMEM((rows * PAIR, width), half),
            pltpu.VMEM((rows * PLANE * PLANES, width), half),
            pltpu.VMEM((PLANE * BLOCK, width), full),
            pltpu.VMEM((PAIR * BLOCK, width), full),
            pltpu.VMEM((PLANE, BLOCK, width), full),
            pltpu.VMEM((PAIR, BLOCK, width), full),
            pltpu.VMEM((PLANE * BLOCK, width), full),
            pltpu.VMEM((PAIR * BLOCK, width), full),
            pltpu.VMEM(right_side.shape, full),
            dma((7 + PLANES,)),
            dma((3,)),
            dma((small,)),
            dma((small,)),
            dma((groups * N_BULK,)),
            dma((groups * N_BULK,)),
            dma((PLANES,)),
            dma((PLANES,)),
        ],
        compiler_params=pltpu.CompilerParams(
            collective_id=0, has_side_effects=True, vmem_limit_bytes=60 * 1024 * 1024
        ),
    )(right_side, inverse_root, inverse_middle, inverse_lower, update_middle, update_lower.T, target_middle, target_lower)


def solution(mesh):
    in_specs = (
        P(("leaf", "sep"), None),
        P(("leaf", "sep"), None),
        P(("leaf", "sep"), None),
        P(("leaf", "sep"), None),
        P(("leaf", "sep"), None),
        P(("leaf", "sep"), None),
        P(("leaf", "sep"), None),
        P(("leaf", "sep"), None),
    )
    out_specs = P(("leaf", "sep"), None)
    fits = dict(mesh.shape) == {"leaf": 8, "sep": 4}
    return jax.shard_map(
        on_device_fused if fits else on_device, mesh=mesh, in_specs=in_specs, out_specs=out_specs, check_vma=False
    )
```

```python
import jax
import jax.numpy as jnp
from jax import lax
from jax.experimental import pallas as pl
from jax.experimental.pallas import tpu as pltpu
from jax.sharding import PartitionSpec as P

BLOCK = 8


def from_partner(block, axis, distance):
    count = lax.axis_size(axis)
    route = []
    for low in range(count):
        high = low | 1 << distance
        if high != low and high < count:
            route += [(low, high), (high, low)]
    return lax.ppermute(block, axis, route)


def on_device(
    right_side,
    inverse_root,
    inverse_middle,
    inverse_lower,
    update_middle,
    update_lower,
    target_middle,
    target_lower,
):
    leaf_index = lax.axis_index("leaf")
    leaf_count = lax.axis_size("leaf")
    leaf_bits = leaf_count.bit_length() - 1
    dev_rows = inverse_root.shape[0]
    width = right_side.shape[1]
    root_side = right_side[:dev_rows]
    middle_side = right_side[dev_rows : 2 * dev_rows]
    lower_side = right_side[2 * dev_rows :]

    def collect(piece, depth_bits):
        panel = lax.all_gather(piece, "sep", axis=0, tiled=True)
        for bit_index in range(depth_bits):
            partner = from_partner(panel, "leaf", bit_index)
            upper = leaf_index >> bit_index & 1 == 1
            first = jnp.where(upper, partner, panel)
            second = jnp.where(upper, panel, partner)
            panel = jnp.concatenate([first, second], axis=0)
        return panel

    def apply_inverse(inverse, words, depth_bits):
        panel = collect(words, depth_bits)
        return jnp.dot(inverse, panel, preferred_element_type=jnp.float32)

    def halve_whole(current, depth_bits):
        for bit_index in reversed(range(depth_bits)):
            half = current.shape[0] // 2
            upper = leaf_index >> bit_index & 1 == 1
            keep = jnp.where(upper, current[half:], current[:half])
            give = jnp.where(upper, current[:half], current[half:])
            current = keep + from_partner(give, "leaf", bit_index)
        return current

    def reduce_slots(partial_value, depth_bits):
        current = halve_whole(partial_value, depth_bits)
        return lax.psum_scatter(current, "sep", scatter_dimension=0, tiled=True)

    def selector(targets, blocks):
        return (jnp.arange(blocks, dtype=jnp.int32)[:, None] == targets[0][None, :]).astype(
            jnp.float32
        )

    def place_slots(summed, targets, blocks):
        onehot = selector(targets, blocks)
        flat = summed.reshape(targets.shape[1], BLOCK * width)
        placed = jnp.dot(onehot, flat, precision=lax.Precision.HIGHEST)
        return placed.reshape(blocks * BLOCK, width)

    def pick_slots(table, targets, blocks):
        onehot = selector(targets, blocks)
        flat = table.astype(jnp.float32).reshape(blocks, BLOCK * width)
        picked = jnp.dot(onehot.T, flat, precision=lax.Precision.HIGHEST)
        return picked.reshape(targets.shape[1] * BLOCK, width).astype(jnp.bfloat16)

    contract_rows = (((0,), (0,)), ((), ()))
    lower_blocks = 2 * dev_rows // BLOCK
    middle_blocks = dev_rows // BLOCK
    lower_words = lower_side.astype(jnp.bfloat16)
    lower_values = apply_inverse(inverse_lower, lower_words, leaf_bits - 2)
    lower_partial = lax.dot_general(
        update_lower, lower_words, contract_rows, preferred_element_type=jnp.float32
    )
    lower_accum = place_slots(
        reduce_slots(lower_partial, leaf_bits - 2), target_lower, lower_blocks
    )
    middle_words = (middle_side - lower_accum[dev_rows:]).astype(jnp.bfloat16)
    middle_values = apply_inverse(inverse_middle, middle_words, leaf_bits - 1)
    middle_partial = lax.dot_general(
        update_middle, middle_words, contract_rows, preferred_element_type=jnp.float32
    )
    middle_accum = place_slots(
        reduce_slots(middle_partial, leaf_bits - 1), target_middle, middle_blocks
    )
    root_words = (root_side - (lower_accum[:dev_rows] + middle_accum)).astype(jnp.bfloat16)
    root_solution = apply_inverse(inverse_root, root_words, leaf_bits)
    root_rounded = root_solution.astype(jnp.bfloat16)
    middle_slots = collect(pick_slots(root_rounded, target_middle, middle_blocks), leaf_bits - 1)
    middle_solution = middle_values - jnp.dot(
        update_middle, middle_slots, preferred_element_type=jnp.float32
    )
    middle_rounded = middle_solution.astype(jnp.bfloat16)
    table = jnp.concatenate([root_rounded, middle_rounded], axis=0)
    lower_slots = collect(pick_slots(table, target_lower, lower_blocks), leaf_bits - 2)
    lower_solution = lower_values - jnp.dot(
        update_lower, lower_slots, preferred_element_type=jnp.float32
    )
    return jnp.concatenate([root_solution, middle_solution, lower_solution], axis=0)


PLANE = 8
PAIR = 16
PLANES = 4
N_BULK = 8
MESH = pl.DeviceIdType.MESH


def fused_kernel(
    side_hbm, root_hbm, middle_hbm, lower_hbm, up_mid_hbm, up_low_hbm, target_mid, target_low, out_hbm,
    side, inv_root, inv_mid, inv_low, up_mid, up_low, low_panel, mid_panel, root_panel,
    low_part, mid_part, low_in, mid_in, hints, slots, xs,
    load_sem, out_sem, small_send, small_recv, bulk_send, bulk_recv, z_send, z_recv,
):
    rows = root_hbm.shape[0]
    plane_cols = PLANE * rows
    leaf, sep = lax.axis_index("leaf"), lax.axis_index("sep")
    z, x, y, c = leaf // 2, leaf % 2, sep // 2, sep % 2
    z1, z2, z3 = z + 1 - 2 * (z % 2), (z + 2) % PLANES, PLANES - 1 - z
    in_plane = x * 4 + sep
    in_pair = (leaf % 4) * 4 + sep

    def plane_peer(step):
        peer = (in_plane + step) % PLANE
        return peer, (z * 2 + peer // 4, peer % 4)

    def pair_peer(step):
        peer = (in_pair + step) % PAIR
        return peer, (leaf // 4 * 4 + peer // 4, peer % 4)

    x_peer = (z * 2 + 1 - x, sep)
    y_peer = (leaf, (1 - y) * 2 + c)
    sibling = (leaf, y * 2 + 1 - c)

    barrier = pltpu.get_barrier_semaphore()
    for step in range(1, PAIR):
        pl.semaphore_signal(barrier, inc=1, device_id=pair_peer(step)[1], device_id_type=MESH)
    for far in (z2, z3):
        pl.semaphore_signal(barrier, inc=1, device_id=(far * 2 + x, sep), device_id_type=MESH)

    loads = [
        pltpu.make_async_copy(side_hbm.at[pl.ds(2 * rows, 2 * rows)], side.at[pl.ds(2 * rows, 2 * rows)], load_sem.at[0]),
        pltpu.make_async_copy(up_low_hbm, up_low, load_sem.at[1]),
        pltpu.make_async_copy(side_hbm.at[pl.ds(0, 2 * rows)], side.at[pl.ds(0, 2 * rows)], load_sem.at[2]),
        pltpu.make_async_copy(up_mid_hbm, up_mid, load_sem.at[3]),
        pltpu.make_async_copy(lower_hbm, inv_low, load_sem.at[4]),
    ]
    for half in range(2):
        loads.append(
            pltpu.make_async_copy(
                middle_hbm.at[:, pl.ds(half * plane_cols, plane_cols)], inv_mid.at[half], load_sem.at[5 + half]
            )
        )
    for plane in range(PLANES):
        loads.append(
            pltpu.make_async_copy(
                root_hbm.at[:, pl.ds(plane * plane_cols, plane_cols)], inv_root.at[plane], load_sem.at[7 + plane]
            )
        )
    for load in loads:
        load.start()

    started = []

    def send(source, target, send_sem, recv_sem, device):
        copy = pltpu.make_async_remote_copy(
            src_ref=source, dst_ref=target, send_sem=send_sem, recv_sem=recv_sem,
            device_id=device, device_id_type=MESH,
        )
        copy.start()
        started.append(copy)

    def arrived(ref, recv_sem):
        pltpu.make_async_remote_copy(
            src_ref=ref, dst_ref=ref, send_sem=small_send.at[0], recv_sem=recv_sem,
            device_id=sibling, device_id_type=MESH,
        ).wait_recv()

    class Gather:
        def __init__(self, panel, size, first, index, across=False):
            self.panel, self.size, self.first, self.index = panel, size, first, index
            self.across = across

        def ref(self, px, py, pc, start=0, size=None):
            where = (self.first + px * 4 + py * 2 + pc) * self.size + start
            return self.panel.at[pl.ds(pl.multiple_of(where, 64), size or self.size)]

        def sems(self, kind):
            place = self.index * N_BULK + kind
            return bulk_send.at[place], bulk_recv.at[place]

        def copy(self, ref, kind, device):
            send(ref, ref, *self.sems(kind), device)

        def wait(self, ref, kind):
            arrived(ref, self.sems(kind)[1])

        def cross(self, ref, place):
            if self.across:
                send(ref, ref, z_send.at[PLANES + place], z_recv.at[PLANES + place], (z1 * 2 + x, sep))

        def crossed(self, px, py, place, kind):
            ref = self.ref(px, py, c)
            arrived(ref, z_recv.at[PLANES + place])
            self.copy(ref, kind, sibling)

        def own(self):
            ref = self.ref(x, y, c)
            self.cross(ref, 0)
            self.copy(ref, 0, x_peer)
            self.copy(ref, 1, y_peer)
            self.copy(ref, 2, sibling)

        def pass_on(self):
            half = self.size // 2
            ref = self.ref(1 - x, y, c)
            self.wait(ref, 0)
            self.copy(self.ref(1 - x, y, c, 0, half), 3, y_peer)
            self.cross(ref, 1)
            self.copy(ref, 5, sibling)
            ref = self.ref(x, 1 - y, c)
            self.wait(ref, 1)
            self.copy(self.ref(x, 1 - y, c, half, half), 4, x_peer)
            self.cross(ref, 2)
            self.copy(ref, 6, sibling)

        def pass_far(self):
            half = self.size // 2
            self.wait(self.ref(1 - x, 1 - y, c, 0, half), 3)
            self.wait(self.ref(1 - x, 1 - y, c, half, half), 4)
            ref = self.ref(1 - x, 1 - y, c)
            self.cross(ref, 3)
            self.copy(ref, 7, sibling)

        def finish(self):
            self.wait(self.ref(x, y, 1 - c), 2)
            self.wait(self.ref(1 - x, y, 1 - c), 5)
            self.wait(self.ref(x, 1 - y, 1 - c), 6)
            self.wait(self.ref(1 - x, 1 - y, 1 - c), 7)

    low = Gather(low_panel, 2 * rows, 0, 0)
    mids = [Gather(mid_panel, rows, (zz % 2) * PLANE, 1 + i, i == 0) for i, zz in enumerate((z, z1))]
    roots = [Gather(root_panel, rows, zz * PLANE, 3 + i) for i, zz in enumerate((z, z1, z2, z3))]

    contract = (((0,), (0,)), ((), ()))

    def spread(block, position):
        wide = jnp.broadcast_to(block[None], (rows // BLOCK,) + block.shape).reshape(rows, block.shape[1])
        place = lax.broadcasted_iota(jnp.int32, wide.shape, 0) // BLOCK
        return jnp.where(place == position, wide, 0.0)

    def pick(table, position):
        blocks = table.reshape(rows // BLOCK, BLOCK, table.shape[1])
        place = lax.broadcasted_iota(jnp.int32, blocks.shape, 0)
        return jnp.sum(jnp.where(place == position, blocks, 0.0), axis=0)

    loads[0].wait()
    loads[1].wait()
    low_words = side[2 * rows :, :].astype(jnp.bfloat16)
    low.ref(x, y, c)[...] = low_words
    low_part[...] = jnp.dot(up_low[...], low_words, preferred_element_type=jnp.float32)
    pl.semaphore_wait(barrier, PAIR - 1 + 2)

    def exchange(part, landing, count, peer_of, base):
        for step in reversed(range(1, count)):
            peer, device = peer_of(step)
            source = part.at[pl.ds(pl.multiple_of(peer * BLOCK, BLOCK), BLOCK)]
            send(source, landing.at[step], small_send.at[base + step], small_recv.at[base + step], device)

    def collected(part, landing, count, mine, base):
        total = part[pl.ds(pl.multiple_of(mine * BLOCK, BLOCK), BLOCK), :]
        for step in range(1, count):
            arrived(landing.at[step], small_recv.at[base + step])
        for step in range(1, count):
            total = total + landing[step]
        return total

    exchange(low_part, low_in, PLANE, plane_peer, 0)
    low.own()
    loads[2].wait()
    loads[3].wait()
    low_sum = collected(low_part, low_in, PLANE, in_plane, 0)

    low_target = target_low[0, 0]
    mid_target = target_mid[0, 0]
    mid_words = (side[rows : 2 * rows, :] - spread(low_sum, low_target - rows // BLOCK)).astype(jnp.bfloat16)
    mids[0].ref(x, y, c)[...] = mid_words
    mid_part[...] = lax.dot_general(up_mid[...], mid_words, contract, preferred_element_type=jnp.float32)
    exchange(mid_part, mid_in, PAIR, pair_peer, PLANE)
    mids[0].own()
    low.pass_on()
    mid_sum = collected(mid_part, mid_in, PAIR, in_pair, PLANE)

    root_words = (side[:rows, :] - (spread(low_sum, low_target) + spread(mid_sum, mid_target))).astype(jnp.bfloat16)
    ref = roots[0].ref(x, y, c)
    ref[...] = root_words
    for i, zz in ((3, z3), (2, z2), (1, z1)):
        send(ref, ref, z_send.at[i], z_recv.at[i], (zz * 2 + x, sep))
    roots[0].own()

    mids[1].crossed(x, y, 0, 2)
    low.pass_far()
    mids[0].pass_on()
    arrived(roots[1].ref(x, y, c), z_recv.at[1])
    roots[1].own()
    low.finish()
    loads[4].wait()

    chunk = 1024
    xs[2 * rows :, :] = jnp.zeros((2 * rows, xs.shape[1]), jnp.float32)

    def low_step(first, last):
        @pl.loop(first, last)
        def _(i):
            start = pl.multiple_of(i * chunk, chunk)
            xs[2 * rows :, :] += jnp.dot(
                inv_low[:, pl.ds(start, chunk)], low_panel[pl.ds(start, chunk), :],
                preferred_element_type=jnp.float32,
            )

    chunks = low_panel.shape[0] // chunk
    low_step(0, chunks // 2)
    mids[0].pass_far()
    arrived(roots[2].ref(x, y, c), z_recv.at[2])
    roots[2].own()
    roots[0].pass_on()
    arrived(roots[3].ref(x, y, c), z_recv.at[3])
    roots[3].own()
    low_step(chunks // 2, chunks)
    mids[1].crossed(1 - x, y, 1, 5)
    mids[1].crossed(x, 1 - y, 2, 6)
    roots[1].pass_on()
    roots[0].pass_far()
    mids[1].crossed(1 - x, 1 - y, 3, 7)
    mids[0].finish()
    mids[1].finish()
    loads[5].wait()
    loads[6].wait()
    xs[rows : 2 * rows, :] = jnp.zeros((rows, xs.shape[1]), jnp.float32)
    xs[:rows, :] = jnp.zeros((rows, xs.shape[1]), jnp.float32)

    def mid_step(half):
        start = half * plane_cols
        xs[rows : 2 * rows, :] += jnp.dot(
            inv_mid[half], mid_panel[start : start + plane_cols, :], preferred_element_type=jnp.float32
        )

    def root_step(gather, plane):
        start = pl.multiple_of(plane * plane_cols, plane_cols)
        xs[:rows, :] += jnp.dot(
            inv_root[plane], root_panel[pl.ds(start, plane_cols), :], preferred_element_type=jnp.float32
        )

    mid_step(0)
    roots[2].pass_on()
    roots[1].pass_far()
    mid_step(1)
    roots[3].pass_on()

    own_hint = hints.at[in_plane]
    own_hint[:BLOCK, :] = pick(xs[rows : 2 * rows, :], low_target - rows // BLOCK)
    own_hint[BLOCK:, :] = pick(up_mid[...].astype(jnp.float32), low_target - rows // BLOCK)
    for step in reversed(range(1, PLANE)):
        at = PLANE + 2 * PAIR + step
        send(own_hint, own_hint, small_send.at[at], small_recv.at[at], plane_peer(step)[1])
    for plane in range(PLANES):
        loads[7 + plane].wait()
    roots[0].finish()
    root_step(roots[0], z)
    roots[2].pass_far()
    roots[1].finish()
    root_step(roots[1], z1)
    roots[3].pass_far()
    roots[2].finish()
    root_step(roots[2], z2)
    roots[3].finish()
    root_step(roots[3], z3)

    def store(piece, start, size):
        copy = pltpu.make_async_copy(xs.at[pl.ds(start, size)], out_hbm.at[pl.ds(start, size)], out_sem.at[piece])
        copy.start()
        return copy

    own_slot = slots.at[in_pair]
    own_slot[:BLOCK, :] = pick(xs[:rows, :], mid_target)
    own_slot[BLOCK:, :] = pick(xs[:rows, :], low_target)
    for step in reversed(range(1, PAIR)):
        at = PLANE + PAIR + step
        send(own_slot, own_slot, small_send.at[at], small_recv.at[at], pair_peer(step)[1])
    stores = [store(0, 0, rows)]
    for step in range(1, PLANE):
        source = (in_plane + PLANE - step) % PLANE
        arrived(hints.at[source], small_recv.at[PLANE + 2 * PAIR + step])
    for step in range(1, PAIR):
        source = (in_pair + PAIR - step) % PAIR
        arrived(slots.at[source], small_recv.at[PLANE + PAIR + step])
    width = xs.shape[1]
    mid_slots = slots[:, :BLOCK, :].reshape(PAIR * BLOCK, width).astype(jnp.bfloat16)
    low_base = slots[pl.ds(in_pair // PLANE * PLANE, PLANE), BLOCK:, :].reshape(PLANE * BLOCK, width)
    hint_value = hints[:, :BLOCK, :].reshape(PLANE * BLOCK, width)
    hint_update = hints[:, BLOCK:, :].reshape(PLANE * BLOCK, width).astype(jnp.bfloat16)
    low_slots = low_base + (hint_value - jnp.dot(hint_update, mid_slots, preferred_element_type=jnp.float32))
    xs[2 * rows :, :] -= lax.dot_general(
        up_low[...], low_slots.astype(jnp.bfloat16), contract, preferred_element_type=jnp.float32
    )
    stores.append(store(2, 2 * rows, 2 * rows))
    xs[rows : 2 * rows, :] -= jnp.dot(up_mid[...], mid_slots, preferred_element_type=jnp.float32)
    stores.append(store(1, rows, rows))
    for copy in started:
        copy.wait_send()
    for copy in stores:
        copy.wait()


def on_device_fused(
    right_side, inverse_root, inverse_middle, inverse_lower, update_middle, update_lower, target_middle, target_lower
):
    rows = inverse_root.shape[0]
    width = right_side.shape[1]
    plane_cols = PLANE * rows
    groups = 1 + 2 + PLANES
    small = 2 * PLANE + 2 * PAIR
    half, full = jnp.bfloat16, jnp.float32
    dma = pltpu.SemaphoreType.DMA
    hbm = pl.BlockSpec(memory_space=pltpu.HBM)
    scalar = pl.BlockSpec(memory_space=pltpu.SMEM)
    return pl.pallas_call(
        fused_kernel,
        out_shape=jax.ShapeDtypeStruct(right_side.shape, full),
        in_specs=[hbm] * 6 + [scalar] * 2,
        out_specs=hbm,
        scratch_shapes=[
            pltpu.VMEM(right_side.shape, full),
            pltpu.VMEM((PLANES, rows, plane_cols), half),
            pltpu.VMEM((2, rows, plane_cols), half),
            pltpu.VMEM(inverse_lower.shape, half),
            pltpu.VMEM(update_middle.shape, half),
            pltpu.VMEM(update_lower.shape[::-1], half),
            pltpu.VMEM((2 * rows * PLANE, width), half),
            pltpu.VMEM((rows * PAIR, width), half),
            pltpu.VMEM((rows * PLANE * PLANES, width), half),
            pltpu.VMEM((PLANE * BLOCK, width), full),
            pltpu.VMEM((PAIR * BLOCK, width), full),
            pltpu.VMEM((PLANE, BLOCK, width), full),
            pltpu.VMEM((PAIR, BLOCK, width), full),
            pltpu.VMEM((PLANE, 2 * BLOCK, width), full),
            pltpu.VMEM((PAIR, 2 * BLOCK, width), full),
            pltpu.VMEM(right_side.shape, full),
            dma((7 + PLANES,)),
            dma((3,)),
            dma((small,)),
            dma((small,)),
            dma((groups * N_BULK,)),
            dma((groups * N_BULK,)),
            dma((2 * PLANES,)),
            dma((2 * PLANES,)),
        ],
        compiler_params=pltpu.CompilerParams(
            collective_id=0, has_side_effects=True, vmem_limit_bytes=60 * 1024 * 1024
        ),
    )(right_side, inverse_root, inverse_middle, inverse_lower, update_middle, update_lower.T, target_middle, target_lower)


def solution(mesh):
    in_specs = (
        P(("leaf", "sep"), None),
        P(("leaf", "sep"), None),
        P(("leaf", "sep"), None),
        P(("leaf", "sep"), None),
        P(("leaf", "sep"), None),
        P(("leaf", "sep"), None),
        P(("leaf", "sep"), None),
        P(("leaf", "sep"), None),
    )
    out_specs = P(("leaf", "sep"), None)
    fits = dict(mesh.shape) == {"leaf": 8, "sep": 4}
    return jax.shard_map(
        on_device_fused if fits else on_device, mesh=mesh, in_specs=in_specs, out_specs=out_specs, check_vma=False
    )
```

```python
import jax
import jax.numpy as jnp
from jax import lax
from jax.experimental import pallas as pl
from jax.experimental.pallas import tpu as pltpu
from jax.sharding import PartitionSpec as P

BLOCK = 8


def from_partner(block, axis, distance):
    count = lax.axis_size(axis)
    route = []
    for low in range(count):
        high = low | 1 << distance
        if high != low and high < count:
            route += [(low, high), (high, low)]
    return lax.ppermute(block, axis, route)


def on_device(
    right_side,
    inverse_root,
    inverse_middle,
    inverse_lower,
    update_middle,
    update_lower,
    target_middle,
    target_lower,
):
    leaf_index = lax.axis_index("leaf")
    leaf_count = lax.axis_size("leaf")
    leaf_bits = leaf_count.bit_length() - 1
    dev_rows = inverse_root.shape[0]
    width = right_side.shape[1]
    root_side = right_side[:dev_rows]
    middle_side = right_side[dev_rows : 2 * dev_rows]
    lower_side = right_side[2 * dev_rows :]

    def collect(piece, depth_bits):
        panel = lax.all_gather(piece, "sep", axis=0, tiled=True)
        for bit_index in range(depth_bits):
            partner = from_partner(panel, "leaf", bit_index)
            upper = leaf_index >> bit_index & 1 == 1
            first = jnp.where(upper, partner, panel)
            second = jnp.where(upper, panel, partner)
            panel = jnp.concatenate([first, second], axis=0)
        return panel

    def apply_inverse(inverse, words, depth_bits):
        panel = collect(words, depth_bits)
        return jnp.dot(inverse, panel, preferred_element_type=jnp.float32)

    def halve_whole(current, depth_bits):
        for bit_index in reversed(range(depth_bits)):
            half = current.shape[0] // 2
            upper = leaf_index >> bit_index & 1 == 1
            keep = jnp.where(upper, current[half:], current[:half])
            give = jnp.where(upper, current[:half], current[half:])
            current = keep + from_partner(give, "leaf", bit_index)
        return current

    def reduce_slots(partial_value, depth_bits):
        current = halve_whole(partial_value, depth_bits)
        return lax.psum_scatter(current, "sep", scatter_dimension=0, tiled=True)

    def selector(targets, blocks):
        return (jnp.arange(blocks, dtype=jnp.int32)[:, None] == targets[0][None, :]).astype(
            jnp.float32
        )

    def place_slots(summed, targets, blocks):
        onehot = selector(targets, blocks)
        flat = summed.reshape(targets.shape[1], BLOCK * width)
        placed = jnp.dot(onehot, flat, precision=lax.Precision.HIGHEST)
        return placed.reshape(blocks * BLOCK, width)

    def pick_slots(table, targets, blocks):
        onehot = selector(targets, blocks)
        flat = table.astype(jnp.float32).reshape(blocks, BLOCK * width)
        picked = jnp.dot(onehot.T, flat, precision=lax.Precision.HIGHEST)
        return picked.reshape(targets.shape[1] * BLOCK, width).astype(jnp.bfloat16)

    contract_rows = (((0,), (0,)), ((), ()))
    lower_blocks = 2 * dev_rows // BLOCK
    middle_blocks = dev_rows // BLOCK
    lower_words = lower_side.astype(jnp.bfloat16)
    lower_values = apply_inverse(inverse_lower, lower_words, leaf_bits - 2)
    lower_partial = lax.dot_general(
        update_lower, lower_words, contract_rows, preferred_element_type=jnp.float32
    )
    lower_accum = place_slots(
        reduce_slots(lower_partial, leaf_bits - 2), target_lower, lower_blocks
    )
    middle_words = (middle_side - lower_accum[dev_rows:]).astype(jnp.bfloat16)
    middle_values = apply_inverse(inverse_middle, middle_words, leaf_bits - 1)
    middle_partial = lax.dot_general(
        update_middle, middle_words, contract_rows, preferred_element_type=jnp.float32
    )
    middle_accum = place_slots(
        reduce_slots(middle_partial, leaf_bits - 1), target_middle, middle_blocks
    )
    root_words = (root_side - (lower_accum[:dev_rows] + middle_accum)).astype(jnp.bfloat16)
    root_solution = apply_inverse(inverse_root, root_words, leaf_bits)
    root_rounded = root_solution.astype(jnp.bfloat16)
    middle_slots = collect(pick_slots(root_rounded, target_middle, middle_blocks), leaf_bits - 1)
    middle_solution = middle_values - jnp.dot(
        update_middle, middle_slots, preferred_element_type=jnp.float32
    )
    middle_rounded = middle_solution.astype(jnp.bfloat16)
    table = jnp.concatenate([root_rounded, middle_rounded], axis=0)
    lower_slots = collect(pick_slots(table, target_lower, lower_blocks), leaf_bits - 2)
    lower_solution = lower_values - jnp.dot(
        update_lower, lower_slots, preferred_element_type=jnp.float32
    )
    return jnp.concatenate([root_solution, middle_solution, lower_solution], axis=0)


PLANE = 8
PAIR = 16
PLANES = 4
N_BULK = 8
MESH = pl.DeviceIdType.MESH


def fused_kernel(
    side_hbm, root_hbm, middle_hbm, lower_hbm, up_mid_hbm, up_low_hbm, target_mid, target_low, out_hbm,
    side, inv_root, inv_mid, inv_low, up_mid, up_low, low_panel, mid_panel, root_panel,
    low_part, mid_part, low_in, mid_in, hints, slots, xs,
    load_sem, out_sem, small_send, small_recv, bulk_send, bulk_recv, z_send, z_recv,
):
    rows = root_hbm.shape[0]
    plane_cols = PLANE * rows
    leaf, sep = lax.axis_index("leaf"), lax.axis_index("sep")
    z, x, y, c = leaf // 2, leaf % 2, sep // 2, sep % 2
    z1, z2, z3 = z + 1 - 2 * (z % 2), (z + 2) % PLANES, PLANES - 1 - z
    in_plane = x * 4 + sep
    in_pair = (leaf % 4) * 4 + sep

    def plane_peer(step):
        peer = (in_plane + step) % PLANE
        return peer, (z * 2 + peer // 4, peer % 4)

    def pair_peer(step):
        peer = (in_pair + step) % PAIR
        return peer, (leaf // 4 * 4 + peer // 4, peer % 4)

    x_peer = (z * 2 + 1 - x, sep)
    y_peer = (leaf, (1 - y) * 2 + c)
    sibling = (leaf, y * 2 + 1 - c)

    barrier = pltpu.get_barrier_semaphore()
    for step in range(1, PAIR):
        pl.semaphore_signal(barrier, inc=1, device_id=pair_peer(step)[1], device_id_type=MESH)
    for far in (z2, z3):
        pl.semaphore_signal(barrier, inc=1, device_id=(far * 2 + x, sep), device_id_type=MESH)

    loads = [
        pltpu.make_async_copy(side_hbm.at[pl.ds(2 * rows, 2 * rows)], side.at[pl.ds(2 * rows, 2 * rows)], load_sem.at[0]),
        pltpu.make_async_copy(up_low_hbm, up_low, load_sem.at[1]),
        pltpu.make_async_copy(side_hbm.at[pl.ds(0, 2 * rows)], side.at[pl.ds(0, 2 * rows)], load_sem.at[2]),
        pltpu.make_async_copy(up_mid_hbm, up_mid, load_sem.at[3]),
        pltpu.make_async_copy(lower_hbm, inv_low, load_sem.at[4]),
    ]
    for half in range(2):
        loads.append(
            pltpu.make_async_copy(
                middle_hbm.at[:, pl.ds(half * plane_cols, plane_cols)], inv_mid.at[half], load_sem.at[5 + half]
            )
        )
    for plane in range(PLANES):
        loads.append(
            pltpu.make_async_copy(
                root_hbm.at[:, pl.ds(plane * plane_cols, plane_cols)], inv_root.at[plane], load_sem.at[7 + plane]
            )
        )
    for load in loads:
        load.start()

    started = []

    def send(source, target, send_sem, recv_sem, device):
        copy = pltpu.make_async_remote_copy(
            src_ref=source, dst_ref=target, send_sem=send_sem, recv_sem=recv_sem,
            device_id=device, device_id_type=MESH,
        )
        copy.start()
        started.append(copy)

    def arrived(ref, recv_sem):
        pltpu.make_async_remote_copy(
            src_ref=ref, dst_ref=ref, send_sem=small_send.at[0], recv_sem=recv_sem,
            device_id=sibling, device_id_type=MESH,
        ).wait_recv()

    class Gather:
        def __init__(self, panel, size, first, index, across=False):
            self.panel, self.size, self.first, self.index = panel, size, first, index
            self.across = across

        def ref(self, px, py, pc, start=0, size=None):
            where = (self.first + px * 4 + py * 2 + pc) * self.size + start
            return self.panel.at[pl.ds(pl.multiple_of(where, 64), size or self.size)]

        def sems(self, kind):
            place = self.index * N_BULK + kind
            return bulk_send.at[place], bulk_recv.at[place]

        def copy(self, ref, kind, device):
            send(ref, ref, *self.sems(kind), device)

        def wait(self, ref, kind):
            arrived(ref, self.sems(kind)[1])

        def cross(self, ref, place):
            if self.across:
                send(ref, ref, z_send.at[PLANES + place], z_recv.at[PLANES + place], (z1 * 2 + x, sep))

        def crossed(self, px, py, place, kind):
            ref = self.ref(px, py, c)
            arrived(ref, z_recv.at[PLANES + place])
            self.copy(ref, kind, sibling)

        def own(self):
            ref = self.ref(x, y, c)
            self.cross(ref, 0)
            self.copy(ref, 0, x_peer)
            self.copy(ref, 1, y_peer)
            self.copy(ref, 2, sibling)

        def pass_on(self):
            half = self.size // 2
            ref = self.ref(1 - x, y, c)
            self.wait(ref, 0)
            self.copy(self.ref(1 - x, y, c, 0, half), 3, y_peer)
            self.cross(ref, 1)
            self.copy(ref, 5, sibling)
            ref = self.ref(x, 1 - y, c)
            self.wait(ref, 1)
            self.copy(self.ref(x, 1 - y, c, half, half), 4, x_peer)
            self.cross(ref, 2)
            self.copy(ref, 6, sibling)

        def pass_far(self):
            half = self.size // 2
            self.wait(self.ref(1 - x, 1 - y, c, 0, half), 3)
            self.wait(self.ref(1 - x, 1 - y, c, half, half), 4)
            ref = self.ref(1 - x, 1 - y, c)
            self.cross(ref, 3)
            self.copy(ref, 7, sibling)

        def finish(self):
            self.wait(self.ref(x, y, 1 - c), 2)
            self.wait(self.ref(1 - x, y, 1 - c), 5)
            self.wait(self.ref(x, 1 - y, 1 - c), 6)
            self.wait(self.ref(1 - x, 1 - y, 1 - c), 7)

    low = Gather(low_panel, 2 * rows, 0, 0)
    mids = [Gather(mid_panel, rows, (zz % 2) * PLANE, 1 + i, i == 0) for i, zz in enumerate((z, z1))]
    roots = [Gather(root_panel, rows, zz * PLANE, 3 + i) for i, zz in enumerate((z, z1, z2, z3))]

    contract = (((0,), (0,)), ((), ()))

    def spread(block, position):
        wide = jnp.broadcast_to(block[None], (rows // BLOCK,) + block.shape).reshape(rows, block.shape[1])
        place = lax.broadcasted_iota(jnp.int32, wide.shape, 0) // BLOCK
        return jnp.where(place == position, wide, 0.0)

    def pick(table, position):
        blocks = table.reshape(rows // BLOCK, BLOCK, table.shape[1])
        place = lax.broadcasted_iota(jnp.int32, blocks.shape, 0)
        return jnp.sum(jnp.where(place == position, blocks, 0.0), axis=0)

    loads[0].wait()
    loads[1].wait()
    low_words = side[2 * rows :, :].astype(jnp.bfloat16)
    low.ref(x, y, c)[...] = low_words
    low_part[...] = jnp.dot(up_low[...], low_words, preferred_element_type=jnp.float32)
    pl.semaphore_wait(barrier, PAIR - 1 + 2)

    def exchange(part, landing, count, peer_of, base):
        for step in reversed(range(1, count)):
            peer, device = peer_of(step)
            source = part.at[pl.ds(pl.multiple_of(peer * BLOCK, BLOCK), BLOCK)]
            send(source, landing.at[step], small_send.at[base + step], small_recv.at[base + step], device)

    def collected(part, landing, count, mine, base):
        total = part[pl.ds(pl.multiple_of(mine * BLOCK, BLOCK), BLOCK), :]
        for step in range(1, count):
            arrived(landing.at[step], small_recv.at[base + step])
        for step in range(1, count):
            total = total + landing[step]
        return total

    exchange(low_part, low_in, PLANE, plane_peer, 0)
    low.own()
    loads[2].wait()
    loads[3].wait()
    low_sum = collected(low_part, low_in, PLANE, in_plane, 0)

    low_target = target_low[0, 0]
    mid_target = target_mid[0, 0]
    mid_words = (side[rows : 2 * rows, :] - spread(low_sum, low_target - rows // BLOCK)).astype(jnp.bfloat16)
    mids[0].ref(x, y, c)[...] = mid_words
    mid_part[...] = lax.dot_general(up_mid[...], mid_words, contract, preferred_element_type=jnp.float32)
    exchange(mid_part, mid_in, PAIR, pair_peer, PLANE)
    mids[0].own()
    low.pass_on()
    mid_sum = collected(mid_part, mid_in, PAIR, in_pair, PLANE)

    root_words = (side[:rows, :] - (spread(low_sum, low_target) + spread(mid_sum, mid_target))).astype(jnp.bfloat16)
    ref = roots[0].ref(x, y, c)
    ref[...] = root_words
    for i, zz in ((1, z1), (2, z2), (3, z3)):
        send(ref, ref, z_send.at[i], z_recv.at[i], (zz * 2 + x, sep))
    roots[0].own()

    mids[1].crossed(x, y, 0, 2)
    low.pass_far()
    mids[0].pass_on()
    arrived(roots[1].ref(x, y, c), z_recv.at[1])
    roots[1].own()
    low.finish()
    loads[4].wait()

    chunk = 1024
    xs[2 * rows :, :] = jnp.zeros((2 * rows, xs.shape[1]), jnp.float32)

    def low_step(first, last):
        @pl.loop(first, last)
        def _(i):
            start = pl.multiple_of(i * chunk, chunk)
            xs[2 * rows :, :] += jnp.dot(
                inv_low[:, pl.ds(start, chunk)], low_panel[pl.ds(start, chunk), :],
                preferred_element_type=jnp.float32,
            )

    chunks = low_panel.shape[0] // chunk
    low_step(0, chunks // 2)
    mids[0].pass_far()
    arrived(roots[2].ref(x, y, c), z_recv.at[2])
    roots[2].own()
    roots[0].pass_on()
    arrived(roots[3].ref(x, y, c), z_recv.at[3])
    roots[3].own()
    low_step(chunks // 2, chunks)
    mids[1].crossed(1 - x, y, 1, 5)
    mids[1].crossed(x, 1 - y, 2, 6)
    roots[1].pass_on()
    roots[0].pass_far()
    mids[1].crossed(1 - x, 1 - y, 3, 7)
    mids[0].finish()
    mids[1].finish()
    loads[5].wait()
    loads[6].wait()
    xs[rows : 2 * rows, :] = jnp.zeros((rows, xs.shape[1]), jnp.float32)
    xs[:rows, :] = jnp.zeros((rows, xs.shape[1]), jnp.float32)

    def mid_step(half):
        start = half * plane_cols
        xs[rows : 2 * rows, :] += jnp.dot(
            inv_mid[half], mid_panel[start : start + plane_cols, :], preferred_element_type=jnp.float32
        )

    def root_step(gather, plane):
        start = pl.multiple_of(plane * plane_cols, plane_cols)
        xs[:rows, :] += jnp.dot(
            inv_root[plane], root_panel[pl.ds(start, plane_cols), :], preferred_element_type=jnp.float32
        )

    mid_step(0)
    roots[2].pass_on()
    roots[1].pass_far()
    mid_step(1)
    roots[3].pass_on()

    own_hint = hints.at[in_plane]
    own_hint[:BLOCK, :] = pick(xs[rows : 2 * rows, :], low_target - rows // BLOCK)
    own_hint[BLOCK:, :] = pick(up_mid[...].astype(jnp.float32), low_target - rows // BLOCK)
    for step in reversed(range(1, PLANE)):
        at = PLANE + 2 * PAIR + step
        send(own_hint, own_hint, small_send.at[at], small_recv.at[at], plane_peer(step)[1])
    for plane in range(PLANES):
        loads[7 + plane].wait()
    roots[0].finish()
    root_step(roots[0], z)
    roots[2].pass_far()
    roots[1].finish()
    root_step(roots[1], z1)
    roots[3].pass_far()
    roots[2].finish()
    root_step(roots[2], z2)
    roots[3].finish()
    root_step(roots[3], z3)

    def store(piece, start, size):
        copy = pltpu.make_async_copy(xs.at[pl.ds(start, size)], out_hbm.at[pl.ds(start, size)], out_sem.at[piece])
        copy.start()
        return copy

    own_slot = slots.at[in_pair]
    own_slot[:BLOCK, :] = pick(xs[:rows, :], mid_target)
    own_slot[BLOCK:, :] = pick(xs[:rows, :], low_target)
    for step in reversed(range(1, PAIR)):
        at = PLANE + PAIR + step
        send(own_slot, own_slot, small_send.at[at], small_recv.at[at], pair_peer(step)[1])
    stores = [store(0, 0, rows)]
    for step in range(1, PLANE):
        source = (in_plane + PLANE - step) % PLANE
        arrived(hints.at[source], small_recv.at[PLANE + 2 * PAIR + step])
    for step in range(1, PAIR):
        source = (in_pair + PAIR - step) % PAIR
        arrived(slots.at[source], small_recv.at[PLANE + PAIR + step])
    width = xs.shape[1]
    mid_slots = slots[:, :BLOCK, :].reshape(PAIR * BLOCK, width).astype(jnp.bfloat16)
    low_base = slots[pl.ds(in_pair // PLANE * PLANE, PLANE), BLOCK:, :].reshape(PLANE * BLOCK, width)
    hint_value = hints[:, :BLOCK, :].reshape(PLANE * BLOCK, width)
    hint_update = hints[:, BLOCK:, :].reshape(PLANE * BLOCK, width).astype(jnp.bfloat16)
    low_slots = low_base + (hint_value - jnp.dot(hint_update, mid_slots, preferred_element_type=jnp.float32))
    xs[2 * rows :, :] -= lax.dot_general(
        up_low[...], low_slots.astype(jnp.bfloat16), contract, preferred_element_type=jnp.float32
    )
    stores.append(store(2, 2 * rows, 2 * rows))
    xs[rows : 2 * rows, :] -= jnp.dot(up_mid[...], mid_slots, preferred_element_type=jnp.float32)
    stores.append(store(1, rows, rows))
    for copy in started:
        copy.wait_send()
    for copy in stores:
        copy.wait()


def on_device_fused(
    right_side, inverse_root, inverse_middle, inverse_lower, update_middle, update_lower, target_middle, target_lower
):
    rows = inverse_root.shape[0]
    width = right_side.shape[1]
    plane_cols = PLANE * rows
    groups = 1 + 2 + PLANES
    small = 2 * PLANE + 2 * PAIR
    half, full = jnp.bfloat16, jnp.float32
    dma = pltpu.SemaphoreType.DMA
    hbm = pl.BlockSpec(memory_space=pltpu.HBM)
    scalar = pl.BlockSpec(memory_space=pltpu.SMEM)
    return pl.pallas_call(
        fused_kernel,
        out_shape=jax.ShapeDtypeStruct(right_side.shape, full),
        in_specs=[hbm] * 6 + [scalar] * 2,
        out_specs=hbm,
        scratch_shapes=[
            pltpu.VMEM(right_side.shape, full),
            pltpu.VMEM((PLANES, rows, plane_cols), half),
            pltpu.VMEM((2, rows, plane_cols), half),
            pltpu.VMEM(inverse_lower.shape, half),
            pltpu.VMEM(update_middle.shape, half),
            pltpu.VMEM(update_lower.shape[::-1], half),
            pltpu.VMEM((2 * rows * PLANE, width), half),
            pltpu.VMEM((rows * PAIR, width), half),
            pltpu.VMEM((rows * PLANE * PLANES, width), half),
            pltpu.VMEM((PLANE * BLOCK, width), full),
            pltpu.VMEM((PAIR * BLOCK, width), full),
            pltpu.VMEM((PLANE, BLOCK, width), full),
            pltpu.VMEM((PAIR, BLOCK, width), full),
            pltpu.VMEM((PLANE, 2 * BLOCK, width), full),
            pltpu.VMEM((PAIR, 2 * BLOCK, width), full),
            pltpu.VMEM(right_side.shape, full),
            dma((7 + PLANES,)),
            dma((3,)),
            dma((small,)),
            dma((small,)),
            dma((groups * N_BULK,)),
            dma((groups * N_BULK,)),
            dma((2 * PLANES,)),
            dma((2 * PLANES,)),
        ],
        compiler_params=pltpu.CompilerParams(
            collective_id=0, has_side_effects=True, vmem_limit_bytes=60 * 1024 * 1024
        ),
    )(right_side, inverse_root, inverse_middle, inverse_lower, update_middle, update_lower.T, target_middle, target_lower)


def solution(mesh):
    in_specs = (
        P(("leaf", "sep"), None),
        P(("leaf", "sep"), None),
        P(("leaf", "sep"), None),
        P(("leaf", "sep"), None),
        P(("leaf", "sep"), None),
        P(("leaf", "sep"), None),
        P(("leaf", "sep"), None),
        P(("leaf", "sep"), None),
    )
    out_specs = P(("leaf", "sep"), None)
    fits = dict(mesh.shape) == {"leaf": 8, "sep": 4}
    return jax.shard_map(
        on_device_fused if fits else on_device, mesh=mesh, in_specs=in_specs, out_specs=out_specs, check_vma=False
    )
```
